32 devices in a mesh: tm: 8 (over y, x, core), space: 4 (over z).
Axes of the slice: x: 2, y: 2, z: 4, core: 2. Of those that a mesh axis runs over, the one named last changes fastest.
Arguments:
- latents: bfloat16 [1, 16, 16, 32, 256], P(None, 'tm', 'space'), may hold values from -24 to 24
- gain_one: float32 [256], replicated, may hold values from 0.25 to 1.75
- conv_one: bfloat16 [3, 3, 3, 256, 256], replicated, may hold values from -0.078125 to 0.078125
- gain_two: float32 [256], replicated, may hold values from 0.25 to 1.75
- conv_two: bfloat16 [3, 3, 3, 256, 256], replicated, may hold values from -0.078125 to 0.078125
- upsample: bfloat16 [3, 256, 256], replicated, may hold values from -0.375 to 0.375
Outputs:
- frames_out: bfloat16 [1, 32, 16, 32, 256], P(None, 'tm', 'space')
The draws below stay inside these ranges and needn't reach their ends.
All inputs are finite; a program needn't handle non-finite values.
Results may differ from the reference program's by a relative error of at most 0.008.
Values may be sent and summed in bfloat16 or wider, within the bound.
A program may use at most 64 MiB of HBM per device.

```python
import math
import jax
import jax.numpy as jnp
from jax import lax

C = 256
V = 1
W = 32
FRAMES = 16
HEIGHT = 16


def draw_latents(key, part):
    key_base, key_cell, key_channel = jax.random.split(key, 3)
    dims_all = (V, FRAMES, HEIGHT, W, C)
    cell_dims = (V, FRAMES, HEIGHT, W, 1)
    base = jnp.clip(jax.random.normal(key_base, dims_all, jnp.float32), -4.0, 4.0)
    cell_scale = jnp.exp(jax.random.uniform(key_cell, cell_dims, jnp.float32, math.log(0.3), math.log(3.0)))
    channel_scale = jnp.exp(jax.random.uniform(key_channel, (C,), jnp.float32, math.log(0.5), math.log(2.0)))
    values = base * cell_scale * channel_scale
    return jnp.clip(values, -24.0, 24.0).astype(jnp.bfloat16)


def bell_draw(own_key, extent, scale, limit, kind=jnp.bfloat16):
    drawn = scale * jax.random.normal(own_key, extent, jnp.float32)
    return jnp.clip(drawn, min=-limit, max=limit).astype(kind)


def setup_inputs(seed: int = 0) -> dict:
    streams_of = jax.random.split(jax.random.key(seed), 7)
    latents = draw_latents(jax.random.fold_in(streams_of[6], 71), 0)
    gain_one = jnp.clip(1.0 + 0.15 * jax.random.normal(streams_of[1], (C,), jnp.float32), 0.25, 1.75)
    conv_one = bell_draw(streams_of[2], (3, 3, 3, C, C), (27 * C) ** -0.5, 0.078125)
    gain_two = jnp.clip(1.0 + 0.15 * jax.random.normal(streams_of[3], (C,), jnp.float32), 0.25, 1.75)
    conv_two = bell_draw(streams_of[4], (3, 3, 3, C, C), (27 * C) ** -0.5, 0.078125)
    upsample = bell_draw(streams_of[5], (3, C, C), C ** -0.5, 0.375)
    return dict(latents=latents, gain_one=gain_one, conv_one=conv_one, gain_two=gain_two, conv_two=conv_two, upsample=upsample)


def normed_silu(features, gain_vec):
    values = features.astype(jnp.float32)
    mean_square = lax.optimization_barrier(jnp.mean(values * values, axis=-1, keepdims=True))
    return jax.nn.silu(values * lax.rsqrt(mean_square + 1e-06) * gain_vec.astype(jnp.float32)).astype(jnp.bfloat16)

def causal_conv(activation, weight):
    padded = jnp.pad(activation.astype(jnp.float32), ((0, 0), (2, 0), (1, 1), (1, 1), (0, 0)))
    return lax.conv_general_dilated(padded, weight.astype(jnp.float32), (1, 1, 1), 'VALID', dimension_numbers=('NDHWC', 'DHWIO', 'NDHWC'), precision=lax.Precision.HIGHEST)

def reference(latents, gain_one, conv_one, gain_two, conv_two, upsample):
    maps = upsample.astype(jnp.float32)

    def decode_video(features):
        first_input = normed_silu(features, gain_one)
        hidden = causal_conv(first_input[None], conv_one)[0].astype(jnp.bfloat16)
        second_input = normed_silu(hidden, gain_two)
        block_out = (features.astype(jnp.float32) + causal_conv(second_input[None], conv_two)[0]).astype(jnp.bfloat16)
        block_f32 = block_out.astype(jnp.float32)
        previous = jnp.concatenate([jnp.zeros((1,) + block_f32.shape[1:], block_f32.dtype), block_f32[:-1]], axis=0)
        even_frames = jnp.einsum('fhwc,cd->fhwd', block_f32, maps[0], precision=lax.Precision.HIGHEST)
        even_frames = even_frames + jnp.einsum('fhwc,cd->fhwd', previous, maps[1], precision=lax.Precision.HIGHEST)
        odd_frames = jnp.einsum('fhwc,cd->fhwd', block_f32, maps[2], precision=lax.Precision.HIGHEST)
        joined = jnp.stack([even_frames, odd_frames], axis=1)
        return joined.reshape((2 * block_f32.shape[0],) + block_f32.shape[1:]).astype(jnp.bfloat16)
    return lax.map(decode_video, latents)
```

```python
import functools

import jax
import jax.numpy as jnp
from jax import lax
from jax.experimental import pallas as pl
from jax.experimental.pallas import tpu as pltpu
from jax.sharding import PartitionSpec as P

MESH = pl.DeviceIdType.MESH
WAYS = ((1, 0), (1, 1), (1, -1), (0, 1), (0, -1))


def normed_silu(values, gain):
    mean_square = jnp.mean(values * values, axis=-1, keepdims=True)
    scaled = values * lax.rsqrt(mean_square + 1e-06) * gain
    return (scaled * jax.nn.sigmoid(scaled)).astype(jnp.bfloat16)


def shifted(total, by, rows, width):
    cells, channels = total.shape
    column = lax.broadcasted_iota(jnp.int32, total.shape, 0) % width
    if by > 0:
        return jnp.where(column == 0, 0.0, pltpu.roll(total, 1, 0))
    return jnp.where(column == width - 1, 0.0, pltpu.roll(total, cells - 1, 0))


def kernel(
    tiles, lat, g1, w1, g2, w2, up, out,
    lbuf, g1buf, g2buf, w1buf, w2buf, ubuf, x1, x2, blocks, previous, obuf,
    load_sem, w1_sem, w2_sem, out_sem, send_sem, recv_sem, last_sem,
):
    T, S = tiles
    _, F, R, W, C = lat.shape
    t, s = lax.axis_index("tm"), lax.axis_index("space")

    loads = [
        pltpu.make_async_copy(lat.at[0], lbuf, load_sem.at[0]),
        pltpu.make_async_copy(g1, g1buf, load_sem.at[1]),
        pltpu.make_async_copy(g2, g2buf, load_sem.at[2]),
        pltpu.make_async_copy(up, ubuf, load_sem.at[3]),
    ]
    w_loads = [
        {dt: pltpu.make_async_copy(w.at[dt], buf.at[dt], sem.at[dt]) for dt in (2, 1, 0)}
        for w, buf, sem in ((w1, w1buf, w1_sem), (w2, w2buf, w2_sem))
    ]
    loads[0].start()
    loads[1].start()
    for dt in (2, 1, 0):
        w_loads[0][dt].start()
    loads[2].start()
    for dt in (2, 1, 0):
        w_loads[1][dt].start()
    loads[3].start()

    def inside(dt, ds):
        checks = []
        if dt > 0:
            checks.append(t < T - 1)
        if dt < 0:
            checks.append(t > 0)
        if ds > 0:
            checks.append(s < S - 1)
        if ds < 0:
            checks.append(s > 0)
        return functools.reduce(jnp.logical_and, checks)

    def there(dt, ds):
        return (t + dt, s + ds)

    barrier = pltpu.get_barrier_semaphore()
    for dt, ds in WAYS:
        @pl.when(inside(-dt, -ds))
        def _():
            pl.semaphore_signal(barrier, inc=1, device_id=there(-dt, -ds), device_id_type=MESH)

    def message(k, x, a, way):
        dt, ds = WAYS[way]
        src_rows = {0: pl.ds(1, R), 1: pl.ds(R, 1), -1: pl.ds(1, 1)}[ds]
        dst_rows = {0: pl.ds(1, R), 1: pl.ds(0, 1), -1: pl.ds(R + 1, 1)}[ds]
        dst_frame = a - (F - 2) if dt else 2 + a
        return pltpu.make_async_remote_copy(
            src_ref=x.at[2 + a, src_rows],
            dst_ref=x.at[dst_frame, dst_rows],
            send_sem=send_sem.at[k, a, way],
            recv_sem=recv_sem.at[k, a, way],
            device_id=there(dt, ds),
            device_id_type=MESH,
        )

    def ways_of(a):
        return [way for way, (dt, _) in enumerate(WAYS) if dt == 0 or a >= F - 2]

    def send(k, x, a):
        for way in ways_of(a):
            @pl.when(inside(*WAYS[way]))
            def _():
                message(k, x, a, way).start()

    def sent(k, x, a):
        for way in ways_of(a):
            @pl.when(inside(*WAYS[way]))
            def _():
                message(k, x, a, way).wait_send()

    arrived = set()

    def receive(k, x, frame):
        if (k, frame) in arrived:
            return
        arrived.add((k, frame))
        early = frame < 2
        a = frame + F - 2 if early else frame - 2
        for way in ways_of(a):
            dt, ds = WAYS[way]
            if (dt > 0) == early:
                @pl.when(inside(-dt, -ds))
                def _():
                    message(k, x, a, way).wait_recv()

    zero_row = jnp.zeros((F + 2, 1, W, C), jnp.bfloat16)
    for x in (x1, x2):
        @pl.when(t == 0)
        def _():
            x[0:2] = jnp.zeros((2, R + 2, W, C), jnp.bfloat16)

        @pl.when(s == 0)
        def _():
            x[:, 0:1] = zero_row

        @pl.when(s == S - 1)
        def _():
            x[:, R + 1 : R + 2] = zero_row

    @pl.when(t == 0)
    def _():
        previous[...] = jnp.zeros((R * W, C), jnp.bfloat16)

    order = list(reversed(range(F)))
    loads[0].wait()
    loads[1].wait()
    for n, a in enumerate(order):
        values = lbuf[a].reshape(R * W, C).astype(jnp.float32)
        x1[2 + a, 1 : R + 1] = normed_silu(values, g1buf[...]).reshape(R, W, C)
        if n == 0:
            targets = sum(inside(*way).astype(jnp.int32) for way in WAYS)
            pl.semaphore_wait(barrier, targets)
        send(0, x1, a)

    loaded = set()

    def conv(k, x, wbuf, a):
        totals = [None] * 3
        for dt in (2, 1, 0):
            if (k, dt) not in loaded:
                loaded.add((k, dt))
                w_loads[k][dt].wait()
            receive(k, x, a + dt)
            cells = jnp.concatenate(
                [x[a + dt, di : di + R].reshape(R * W, C) for di in range(3)], axis=1
            )
            for dj in range(3):
                taps = jnp.concatenate([wbuf[dt, di, dj] for di in range(3)], axis=0)
                part = jnp.dot(cells, taps, preferred_element_type=jnp.float32)
                totals[dj] = part if totals[dj] is None else totals[dj] + part
        return shifted(totals[0], 1, R, W) + totals[1] + shifted(totals[2], -1, R, W)

    for n, a in enumerate(order):
        hidden = conv(0, x1, w1buf, a).astype(jnp.bfloat16).astype(jnp.float32)
        if n == 0:
            loads[2].wait()
        x2[2 + a, 1 : R + 1] = normed_silu(hidden, g2buf[...]).reshape(R, W, C)
        send(1, x2, a)

    last = pltpu.make_async_remote_copy(
        src_ref=blocks.at[F - 1], dst_ref=previous,
        send_sem=last_sem.at[0], recv_sem=last_sem.at[1],
        device_id=there(1, 0), device_id_type=MESH,
    )
    for n, a in enumerate(order):
        total = conv(1, x2, w2buf, a) + lbuf[a].reshape(R * W, C).astype(jnp.float32)
        blocks[a] = total.astype(jnp.bfloat16)
        if n == 0:
            @pl.when(inside(1, 0))
            def _():
                last.start()

    loads[3].wait()
    stores = [pltpu.make_async_copy(obuf.at[j], out.at[0, j], out_sem.at[j]) for j in range(2 * F)]

    def put(j, value):
        obuf[j] = value.astype(jnp.bfloat16).reshape(R, W, C)
        stores[j].start()

    def product(rows, m):
        return jnp.dot(rows, ubuf[m], preferred_element_type=jnp.float32)

    for a in order:
        put(2 * a + 1, product(blocks[a], 2))
        if a:
            put(2 * a, product(blocks[a], 0) + product(blocks[a - 1], 1))
    first = product(blocks[0], 0)

    @pl.when(inside(-1, 0))
    def _():
        last.wait_recv()

    put(0, first + product(previous[...], 1))

    for k, x in enumerate((x1, x2)):
        for a in order:
            sent(k, x, a)

    @pl.when(inside(1, 0))
    def _():
        last.wait_send()

    for store in stores:
        store.wait()


def local(tiles, latents, gain_one, conv_one, gain_two, conv_two, upsample):
    videos, F, R, W, C = latents.shape
    assert videos == 1 and F >= 2
    anywhere = pl.BlockSpec(memory_space=pl.ANY)
    in_hbm = pl.BlockSpec(memory_space=pltpu.HBM)
    bf16, f32 = jnp.bfloat16, jnp.float32
    return pl.pallas_call(
        functools.partial(kernel, tiles),
        out_shape=jax.ShapeDtypeStruct((1, 2 * F, R, W, C), bf16),
        in_specs=[in_hbm] * 6,
        out_specs=anywhere,
        scratch_shapes=[
            pltpu.VMEM((F, R, W, C), bf16),
            pltpu.VMEM((1, C), f32),
            pltpu.VMEM((1, C), f32),
            pltpu.VMEM(conv_one.shape, bf16),
            pltpu.VMEM(conv_two.shape, bf16),
            pltpu.VMEM(upsample.shape, bf16),
            pltpu.VMEM((F + 2, R + 2, W, C), bf16),
            pltpu.VMEM((F + 2, R + 2, W, C), bf16),
            pltpu.VMEM((F, R * W, C), bf16),
            pltpu.VMEM((R * W, C), bf16),
            pltpu.VMEM((2 * F, R, W, C), bf16),
            pltpu.SemaphoreType.DMA((4,)),
            pltpu.SemaphoreType.DMA((3,)),
            pltpu.SemaphoreType.DMA((3,)),
            pltpu.SemaphoreType.DMA((2 * F,)),
            pltpu.SemaphoreType.DMA((2, F, len(WAYS))),
            pltpu.SemaphoreType.DMA((2, F, len(WAYS))),
            pltpu.SemaphoreType.DMA((2,)),
        ],
        compiler_params=pltpu.CompilerParams(
            collective_id=0, has_side_effects=True, vmem_limit_bytes=56 * 2**20
        ),
        cost_estimate=pl.CostEstimate(
            flops=2 * F * R * W * C * C * 57, bytes_accessed=8 * 2**20, transcendentals=4 * F * R * W * C
        ),
    )(latents, gain_one.reshape(1, C), conv_one, gain_two.reshape(1, C), conv_two, upsample)


def solution(mesh):
    tiles = (mesh.shape["tm"], mesh.shape["space"])
    return jax.shard_map(
        functools.partial(local, tiles),
        mesh=mesh,
        in_specs=(P(None, "tm", "space", None, None), P(), P(), P(), P(), P()),
        out_specs=P(None, "tm", "space", None, None),
        check_vma=False,
    )
```

```python
import functools

import jax
import jax.numpy as jnp
from jax import lax
from jax.experimental import pallas as pl
from jax.experimental.pallas import tpu as pltpu
from jax.sharding import PartitionSpec as P

MESH = pl.DeviceIdType.MESH
WAYS = ((1, 0), (1, 1), (1, -1), (0, 1), (0, -1))


def normed_silu(values, gain):
    mean_square = jnp.mean(values * values, axis=-1, keepdims=True)
    scaled = values * lax.rsqrt(mean_square + 1e-06) * gain
    return (scaled * jax.nn.sigmoid(scaled)).astype(jnp.bfloat16)


def shifted(total, by, rows, width):
    cells, channels = total.shape
    column = lax.broadcasted_iota(jnp.int32, total.shape, 0) % width
    if by > 0:
        return jnp.where(column == 0, 0.0, pltpu.roll(total, 1, 0))
    return jnp.where(column == width - 1, 0.0, pltpu.roll(total, cells - 1, 0))


def kernel(
    tiles, lat, g1, w1, g2, w2, up, out,
    lbuf, g1buf, g2buf, w1buf, w2buf, ubuf, x1, x2, blocks, previous,
    load_sem, w1_sem, w2_sem, send_sem, recv_sem, last_sem,
):
    T, S = tiles
    _, F, R, W, C = lat.shape
    t, s = lax.axis_index("tm"), lax.axis_index("space")

    loads = [
        pltpu.make_async_copy(lat.at[0], lbuf, load_sem.at[0]),
        pltpu.make_async_copy(g1, g1buf, load_sem.at[1]),
        pltpu.make_async_copy(g2, g2buf, load_sem.at[2]),
        pltpu.make_async_copy(up, ubuf, load_sem.at[3]),
    ]
    w_loads = [
        {dt: pltpu.make_async_copy(w.at[dt], buf.at[dt], sem.at[dt]) for dt in (2, 1, 0)}
        for w, buf, sem in ((w1, w1buf, w1_sem), (w2, w2buf, w2_sem))
    ]
    loads[0].start()
    loads[1].start()
    for dt in (2, 1, 0):
        w_loads[0][dt].start()
    loads[2].start()
    for dt in (2, 1, 0):
        w_loads[1][dt].start()
    loads[3].start()

    def inside(dt, ds):
        checks = []
        if dt > 0:
            checks.append(t < T - 1)
        if dt < 0:
            checks.append(t > 0)
        if ds > 0:
            checks.append(s < S - 1)
        if ds < 0:
            checks.append(s > 0)
        return functools.reduce(jnp.logical_and, checks)

    def there(dt, ds):
        return (t + dt, s + ds)

    barrier = pltpu.get_barrier_semaphore()
    for dt, ds in WAYS:
        @pl.when(inside(-dt, -ds))
        def _():
            pl.semaphore_signal(barrier, inc=1, device_id=there(-dt, -ds), device_id_type=MESH)

    def message(k, x, a, way):
        dt, ds = WAYS[way]
        src_rows = {0: pl.ds(1, R), 1: pl.ds(R, 1), -1: pl.ds(1, 1)}[ds]
        dst_rows = {0: pl.ds(1, R), 1: pl.ds(0, 1), -1: pl.ds(R + 1, 1)}[ds]
        dst_frame = a - (F - 2) if dt else 2 + a
        return pltpu.make_async_remote_copy(
            src_ref=x.at[2 + a, src_rows],
            dst_ref=x.at[dst_frame, dst_rows],
            send_sem=send_sem.at[k, a, way],
            recv_sem=recv_sem.at[k, a, way],
            device_id=there(dt, ds),
            device_id_type=MESH,
        )

    def ways_of(a):
        return [way for way, (dt, _) in enumerate(WAYS) if dt == 0 or a >= F - 2]

    def send(k, x, a):
        for way in ways_of(a):
            @pl.when(inside(*WAYS[way]))
            def _():
                message(k, x, a, way).start()

    def sent(k, x, a):
        for way in ways_of(a):
            @pl.when(inside(*WAYS[way]))
            def _():
                message(k, x, a, way).wait_send()

    arrived = set()

    def receive(k, x, frame):
        if (k, frame) in arrived:
            return
        arrived.add((k, frame))
        early = frame < 2
        a = frame + F - 2 if early else frame - 2
        for way in ways_of(a):
            dt, ds = WAYS[way]
            if (dt > 0) == early:
                @pl.when(inside(-dt, -ds))
                def _():
                    message(k, x, a, way).wait_recv()

    zero_row = jnp.zeros((F + 2, 1, W, C), jnp.bfloat16)
    for x in (x1, x2):
        @pl.when(t == 0)
        def _():
            x[0:2] = jnp.zeros((2, R + 2, W, C), jnp.bfloat16)

        @pl.when(s == 0)
        def _():
            x[:, 0:1] = zero_row

        @pl.when(s == S - 1)
        def _():
            x[:, R + 1 : R + 2] = zero_row

    @pl.when(t == 0)
    def _():
        previous[...] = jnp.zeros((R * W, C), jnp.bfloat16)

    order = list(reversed(range(F)))
    loads[0].wait()
    loads[1].wait()
    for n, a in enumerate(order):
        values = lbuf[a].reshape(R * W, C).astype(jnp.float32)
        x1[2 + a, 1 : R + 1] = normed_silu(values, g1buf[...]).reshape(R, W, C)
        if n == 0:
            targets = sum(inside(*way).astype(jnp.int32) for way in WAYS)
            pl.semaphore_wait(barrier, targets)
        send(0, x1, a)

    loaded = set()

    def conv(k, x, wbuf, a):
        totals = [None] * 3
        for dt in (2, 1, 0):
            if (k, dt) not in loaded:
                loaded.add((k, dt))
                w_loads[k][dt].wait()
            receive(k, x, a + dt)
            cells = jnp.concatenate(
                [x[a + dt, di : di + R].reshape(R * W, C) for di in range(3)], axis=1
            )
            for dj in range(3):
                taps = jnp.concatenate([wbuf[dt, di, dj] for di in range(3)], axis=0)
                part = jnp.dot(cells, taps, preferred_element_type=jnp.float32)
                totals[dj] = part if totals[dj] is None else totals[dj] + part
        return shifted(totals[0], 1, R, W) + totals[1] + shifted(totals[2], -1, R, W)

    for n, a in enumerate(order):
        hidden = conv(0, x1, w1buf, a).astype(jnp.bfloat16).astype(jnp.float32)
        if n == 0:
            loads[2].wait()
        x2[2 + a, 1 : R + 1] = normed_silu(hidden, g2buf[...]).reshape(R, W, C)
        send(1, x2, a)

    last = pltpu.make_async_remote_copy(
        src_ref=blocks.at[F - 1], dst_ref=previous,
        send_sem=last_sem.at[0], recv_sem=last_sem.at[1],
        device_id=there(1, 0), device_id_type=MESH,
    )
    for n, a in enumerate(order):
        total = conv(1, x2, w2buf, a) + lbuf[a].reshape(R * W, C).astype(jnp.float32)
        blocks[a] = total.astype(jnp.bfloat16)
        if n == 0:
            @pl.when(inside(1, 0))
            def _():
                last.start()

    loads[3].wait()

    def put(j, value):
        out[0, j] = value.astype(jnp.bfloat16).reshape(R, W, C)

    def product(rows, m):
        return jnp.dot(rows, ubuf[m], preferred_element_type=jnp.float32)

    for a in order:
        put(2 * a + 1, product(blocks[a], 2))
        if a:
            put(2 * a, product(blocks[a], 0) + product(blocks[a - 1], 1))
    first = product(blocks[0], 0)

    @pl.when(inside(-1, 0))
    def _():
        last.wait_recv()

    put(0, first + product(previous[...], 1))

    for k, x in enumerate((x1, x2)):
        for a in order:
            sent(k, x, a)

    @pl.when(inside(1, 0))
    def _():
        last.wait_send()


def local(tiles, latents, gain_one, conv_one, gain_two, conv_two, upsample):
    videos, F, R, W, C = latents.shape
    assert videos == 1 and F >= 2
    in_hbm = pl.BlockSpec(memory_space=pltpu.HBM)
    bf16, f32 = jnp.bfloat16, jnp.float32
    return pl.pallas_call(
        functools.partial(kernel, tiles),
        out_shape=pltpu.VMEM((1, 2 * F, R, W, C), bf16),
        in_specs=[in_hbm] * 6,
        out_specs=pl.BlockSpec(memory_space=pltpu.VMEM),
        scratch_shapes=[
            pltpu.VMEM((F, R, W, C), bf16),
            pltpu.VMEM((1, C), f32),
            pltpu.VMEM((1, C), f32),
            pltpu.VMEM(conv_one.shape, bf16),
            pltpu.VMEM(conv_two.shape, bf16),
            pltpu.VMEM(upsample.shape, bf16),
            pltpu.VMEM((F + 2, R + 2, W, C), bf16),
            pltpu.VMEM((F + 2, R + 2, W, C), bf16),
            pltpu.VMEM((F, R * W, C), bf16),
            pltpu.VMEM((R * W, C), bf16),
            pltpu.SemaphoreType.DMA((4,)),
            pltpu.SemaphoreType.DMA((3,)),
            pltpu.SemaphoreType.DMA((3,)),
            pltpu.SemaphoreType.DMA((2, F, len(WAYS))),
            pltpu.SemaphoreType.DMA((2, F, len(WAYS))),
            pltpu.SemaphoreType.DMA((2,)),
        ],
        compiler_params=pltpu.CompilerParams(
            collective_id=0, has_side_effects=True, vmem_limit_bytes=56 * 2**20
        ),
        cost_estimate=pl.CostEstimate(
            flops=2 * F * R * W * C * C * 57, bytes_accessed=8 * 2**20, transcendentals=4 * F * R * W * C
        ),
    )(latents, gain_one.reshape(1, C), conv_one, gain_two.reshape(1, C), conv_two, upsample)


def solution(mesh):
    tiles = (mesh.shape["tm"], mesh.shape["space"])
    return jax.shard_map(
        functools.partial(local, tiles),
        mesh=mesh,
        in_specs=(P(None, "tm", "space", None, None), P(), P(), P(), P(), P()),
        out_specs=P(None, "tm", "space", None, None),
        check_vma=False,
    )
```

```python
import functools

import jax
import jax.numpy as jnp
from jax import lax
from jax.experimental import pallas as pl
from jax.experimental.pallas import tpu as pltpu
from jax.sharding import PartitionSpec as P

MESH = pl.DeviceIdType.MESH
WAYS = ((0, 1), (0, -1), (1, 0), (1, 1), (1, -1))


def normed_silu(values, gain):
    mean_square = jnp.mean(values * values, axis=-1, keepdims=True)
    scaled = values * lax.rsqrt(mean_square + 1e-06) * gain
    return (scaled * jax.nn.sigmoid(scaled)).astype(jnp.bfloat16)


def shifted(total, by, rows, width):
    cells, channels = total.shape
    column = lax.broadcasted_iota(jnp.int32, total.shape, 0) % width
    if by > 0:
        return jnp.where(column == 0, 0.0, pltpu.roll(total, 1, 0))
    return jnp.where(column == width - 1, 0.0, pltpu.roll(total, cells - 1, 0))


def kernel(
    tiles, lat, g1, w1, g2, w2, up, out,
    lbuf, g1buf, g2buf, w1buf, w2buf, ubuf, x1, x2, blocks, previous,
    load_sem, w1_sem, w2_sem, send_sem, recv_sem, last_sem,
):
    T, S = tiles
    _, F, R, W, C = lat.shape
    t, s = lax.axis_index("tm"), lax.axis_index("space")

    loads = [
        pltpu.make_async_copy(lat.at[0], lbuf, load_sem.at[0]),
        pltpu.make_async_copy(g1, g1buf, load_sem.at[1]),
        pltpu.make_async_copy(g2, g2buf, load_sem.at[2]),
        pltpu.make_async_copy(up, ubuf, load_sem.at[3]),
    ]
    w_loads = [
        {dt: pltpu.make_async_copy(w.at[dt], buf.at[dt], sem.at[dt]) for dt in (2, 1, 0)}
        for w, buf, sem in ((w1, w1buf, w1_sem), (w2, w2buf, w2_sem))
    ]
    loads[0].start()
    loads[1].start()
    for dt in (2, 1, 0):
        w_loads[0][dt].start()
    loads[2].start()
    for dt in (2, 1, 0):
        w_loads[1][dt].start()
    loads[3].start()

    def inside(dt, ds):
        checks = []
        if dt > 0:
            checks.append(t < T - 1)
        if dt < 0:
            checks.append(t > 0)
        if ds > 0:
            checks.append(s < S - 1)
        if ds < 0:
            checks.append(s > 0)
        return functools.reduce(jnp.logical_and, checks)

    def there(dt, ds):
        return (t + dt, s + ds)

    barrier = pltpu.get_barrier_semaphore()
    for dt, ds in WAYS:
        @pl.when(inside(-dt, -ds))
        def _():
            pl.semaphore_signal(barrier, inc=1, device_id=there(-dt, -ds), device_id_type=MESH)

    def message(k, x, a, way):
        dt, ds = WAYS[way]
        src_rows = {0: pl.ds(1, R), 1: pl.ds(R, 1), -1: pl.ds(1, 1)}[ds]
        dst_rows = {0: pl.ds(1, R), 1: pl.ds(0, 1), -1: pl.ds(R + 1, 1)}[ds]
        dst_frame = a - (F - 2) if dt else 2 + a
        return pltpu.make_async_remote_copy(
            src_ref=x.at[2 + a, src_rows],
            dst_ref=x.at[dst_frame, dst_rows],
            send_sem=send_sem.at[k, a, way],
            recv_sem=recv_sem.at[k, a, way],
            device_id=there(dt, ds),
            device_id_type=MESH,
        )

    def ways_of(a):
        return [way for way, (dt, _) in enumerate(WAYS) if dt == 0 or a >= F - 2]

    def send(k, x, a):
        for way in ways_of(a):
            @pl.when(inside(*WAYS[way]))
            def _():
                message(k, x, a, way).start()

    def sent(k, x, a):
        for way in ways_of(a):
            @pl.when(inside(*WAYS[way]))
            def _():
                message(k, x, a, way).wait_send()

    arrived = set()

    def receive(k, x, frame):
        if (k, frame) in arrived:
            return
        arrived.add((k, frame))
        early = frame < 2
        a = frame + F - 2 if early else frame - 2
        for way in ways_of(a):
            dt, ds = WAYS[way]
            if (dt > 0) == early:
                @pl.when(inside(-dt, -ds))
                def _():
                    message(k, x, a, way).wait_recv()

    zero_row = jnp.zeros((F + 2, 1, W, C), jnp.bfloat16)
    for x in (x1, x2):
        @pl.when(t == 0)
        def _():
            x[0:2] = jnp.zeros((2, R + 2, W, C), jnp.bfloat16)

        @pl.when(s == 0)
        def _():
            x[:, 0:1] = zero_row

        @pl.when(s == S - 1)
        def _():
            x[:, R + 1 : R + 2] = zero_row

    @pl.when(t == 0)
    def _():
        previous[...] = jnp.zeros((R * W, C), jnp.bfloat16)

    order = list(reversed(range(F)))
    loads[0].wait()
    loads[1].wait()
    for n, a in enumerate(order):
        values = lbuf[a].reshape(R * W, C).astype(jnp.float32)
        x1[2 + a, 1 : R + 1] = normed_silu(values, g1buf[...]).reshape(R, W, C)
        if n == 0:
            targets = sum(inside(*way).astype(jnp.int32) for way in WAYS)
            pl.semaphore_wait(barrier, targets)
        send(0, x1, a)

    loaded = set()

    def conv(k, x, wbuf):
        totals = {}

        def add(frames, dt):
            if (k, dt) not in loaded:
                loaded.add((k, dt))
                w_loads[k][dt].wait()
            low, count = frames[0], len(frames)
            for a in frames:
                receive(k, x, a + dt)
            cells = jnp.concatenate(
                [
                    x[low + dt : low + dt + count, di : di + R].reshape(count * R * W, C)
                    for di in range(3)
                ],
                axis=1,
            )
            for dj in range(3):
                taps = jnp.concatenate([wbuf[dt, di, dj] for di in range(3)], axis=0)
                part = jnp.dot(cells, taps, preferred_element_type=jnp.float32)
                for n, a in enumerate(frames):
                    piece = part[n * R * W : (n + 1) * R * W]
                    totals[a, dj] = totals[a, dj] + piece if (a, dj) in totals else piece

        for dt in (2, 1, 0):
            frames = [a for a in range(F) if a + dt >= 2]
            if frames:
                add(frames, dt)
        for a in order:
            for dt in (1, 0):
                if a + dt < 2:
                    add([a], dt)
            yield a, shifted(totals[a, 0], 1, R, W) + totals[a, 1] + shifted(totals[a, 2], -1, R, W)

    for a, total in conv(0, x1, w1buf):
        hidden = total.astype(jnp.bfloat16).astype(jnp.float32)
        if a == F - 1:
            loads[2].wait()
        x2[2 + a, 1 : R + 1] = normed_silu(hidden, g2buf[...]).reshape(R, W, C)
        send(1, x2, a)

    last = pltpu.make_async_remote_copy(
        src_ref=blocks.at[F - 1], dst_ref=previous,
        send_sem=last_sem.at[0], recv_sem=last_sem.at[1],
        device_id=there(1, 0), device_id_type=MESH,
    )
    for a, total in conv(1, x2, w2buf):
        total = total + lbuf[a].reshape(R * W, C).astype(jnp.float32)
        blocks[a] = total.astype(jnp.bfloat16)
        if a == F - 1:
            @pl.when(inside(1, 0))
            def _():
                last.start()

    loads[3].wait()

    def put(j, value):
        out[0, j] = value.astype(jnp.bfloat16).reshape(R, W, C)

    def product(rows, m):
        return jnp.dot(rows, ubuf[m], preferred_element_type=jnp.float32)

    for a in order:
        put(2 * a + 1, product(blocks[a], 2))
        if a:
            put(2 * a, product(blocks[a], 0) + product(blocks[a - 1], 1))
    first = product(blocks[0], 0)

    @pl.when(inside(-1, 0))
    def _():
        last.wait_recv()

    put(0, first + product(previous[...], 1))

    for k, x in enumerate((x1, x2)):
        for a in order:
            sent(k, x, a)

    @pl.when(inside(1, 0))
    def _():
        last.wait_send()


def local(tiles, latents, gain_one, conv_one, gain_two, conv_two, upsample):
    videos, F, R, W, C = latents.shape
    assert videos == 1 and F >= 2
    in_hbm = pl.BlockSpec(memory_space=pltpu.HBM)
    bf16, f32 = jnp.bfloat16, jnp.float32
    return pl.pallas_call(
        functools.partial(kernel, tiles),
        out_shape=pltpu.VMEM((1, 2 * F, R, W, C), bf16),
        in_specs=[in_hbm] * 6,
        out_specs=pl.BlockSpec(memory_space=pltpu.VMEM),
        scratch_shapes=[
            pltpu.VMEM((F, R, W, C), bf16),
            pltpu.VMEM((1, C), f32),
            pltpu.VMEM((1, C), f32),
            pltpu.VMEM(conv_one.shape, bf16),
            pltpu.VMEM(conv_two.shape, bf16),
            pltpu.VMEM(upsample.shape, bf16),
            pltpu.VMEM((F + 2, R + 2, W, C), bf16),
            pltpu.VMEM((F + 2, R + 2, W, C), bf16),
            pltpu.VMEM((F, R * W, C), bf16),
            pltpu.VMEM((R * W, C), bf16),
            pltpu.SemaphoreType.DMA((4,)),
            pltpu.SemaphoreType.DMA((3,)),
            pltpu.SemaphoreType.DMA((3,)),
            pltpu.SemaphoreType.DMA((2, F, len(WAYS))),
            pltpu.SemaphoreType.DMA((2, F, len(WAYS))),
            pltpu.SemaphoreType.DMA((2,)),
        ],
        compiler_params=pltpu.CompilerParams(
            collective_id=0, has_side_effects=True, vmem_limit_bytes=56 * 2**20
        ),
        cost_estimate=pl.CostEstimate(
            flops=2 * F * R * W * C * C * 57, bytes_accessed=8 * 2**20, transcendentals=4 * F * R * W * C
        ),
    )(latents, gain_one.reshape(1, C), conv_one, gain_two.reshape(1, C), conv_two, upsample)


def solution(mesh):
    tiles = (mesh.shape["tm"], mesh.shape["space"])
    return jax.shard_map(
        functools.partial(local, tiles),
        mesh=mesh,
        in_specs=(P(None, "tm", "space", None, None), P(), P(), P(), P(), P()),
        out_specs=P(None, "tm", "space", None, None),
        check_vma=False,
    )
```

```python
import functools

import jax
import jax.numpy as jnp
from jax import lax
from jax.experimental import pallas as pl
from jax.experimental.pallas import tpu as pltpu
from jax.sharding import PartitionSpec as P

MESH = pl.DeviceIdType.MESH
WAYS = ((1, 0), (1, 1), (1, -1), (0, 1), (0, -1))


def normed_silu(values, gain):
    mean_square = jnp.mean(values * values, axis=-1, keepdims=True)
    scaled = values * lax.rsqrt(mean_square + 1e-06) * gain
    return (scaled * jax.nn.sigmoid(scaled)).astype(jnp.bfloat16)


def shifted(total, by, rows, width):
    cells, channels = total.shape
    column = lax.broadcasted_iota(jnp.int32, total.shape, 0) % width
    if by > 0:
        return jnp.where(column == 0, 0.0, pltpu.roll(total, 1, 0))
    return jnp.where(column == width - 1, 0.0, pltpu.roll(total, cells - 1, 0))


def kernel(
    tiles, lat, g1, w1, g2, w2, up, out,
    lbuf, g1buf, g2buf, w1buf, w2buf, ubuf, x1, x2, blocks, previous,
    load_sem, w1_sem, w2_sem, send_sem, recv_sem, last_sem,
):
    T, S = tiles
    _, F, R, W, C = lat.shape
    t, s = lax.axis_index("tm"), lax.axis_index("space")

    loads = [
        pltpu.make_async_copy(lat.at[0], lbuf, load_sem.at[0]),
        pltpu.make_async_copy(g1, g1buf, load_sem.at[1]),
        pltpu.make_async_copy(g2, g2buf, load_sem.at[2]),
        pltpu.make_async_copy(up, ubuf, load_sem.at[3]),
    ]
    w_loads = [
        {dt: pltpu.make_async_copy(w.at[dt], buf.at[dt], sem.at[dt]) for dt in (2, 1, 0)}
        for w, buf, sem in ((w1, w1buf, w1_sem), (w2, w2buf, w2_sem))
    ]
    loads[0].start()
    loads[1].start()
    for dt in (2, 1, 0):
        w_loads[0][dt].start()
    loads[2].start()

    def inside(dt, ds):
        checks = []
        if dt > 0:
            checks.append(t < T - 1)
        if dt < 0:
            checks.append(t > 0)
        if ds > 0:
            checks.append(s < S - 1)
        if ds < 0:
            checks.append(s > 0)
        return functools.reduce(jnp.logical_and, checks)

    def there(dt, ds):
        return (t + dt, s + ds)

    barrier = pltpu.get_barrier_semaphore()
    for dt, ds in WAYS:
        @pl.when(inside(-dt, -ds))
        def _():
            pl.semaphore_signal(barrier, inc=1, device_id=there(-dt, -ds), device_id_type=MESH)

    def message(k, x, a, way):
        dt, ds = WAYS[way]
        src_rows = {0: pl.ds(1, R), 1: pl.ds(R, 1), -1: pl.ds(1, 1)}[ds]
        dst_rows = {0: pl.ds(1, R), 1: pl.ds(0, 1), -1: pl.ds(R + 1, 1)}[ds]
        dst_frame = a - (F - 2) if dt else 2 + a
        return pltpu.make_async_remote_copy(
            src_ref=x.at[2 + a, src_rows],
            dst_ref=x.at[dst_frame, dst_rows],
            send_sem=send_sem.at[k, a, way],
            recv_sem=recv_sem.at[k, a, way],
            device_id=there(dt, ds),
            device_id_type=MESH,
        )

    def ways_of(a):
        return [way for way, (dt, _) in enumerate(WAYS) if dt == 0 or a >= F - 2]

    def send(k, x, a):
        for way in ways_of(a):
            @pl.when(inside(*WAYS[way]))
            def _():
                message(k, x, a, way).start()

    def sent(k, x, a):
        for way in ways_of(a):
            @pl.when(inside(*WAYS[way]))
            def _():
                message(k, x, a, way).wait_send()

    arrived = set()

    def receive(k, x, frame):
        if (k, frame) in arrived:
            return
        arrived.add((k, frame))
        early = frame < 2
        a = frame + F - 2 if early else frame - 2
        for way in ways_of(a):
            dt, ds = WAYS[way]
            if (dt > 0) == early:
                @pl.when(inside(-dt, -ds))
                def _():
                    message(k, x, a, way).wait_recv()

    zero_row = jnp.zeros((F + 2, 1, W, C), jnp.bfloat16)
    for x in (x1, x2):
        @pl.when(t == 0)
        def _():
            x[0:2] = jnp.zeros((2, R + 2, W, C), jnp.bfloat16)

        @pl.when(s == 0)
        def _():
            x[:, 0:1] = zero_row

        @pl.when(s == S - 1)
        def _():
            x[:, R + 1 : R + 2] = zero_row

    @pl.when(t == 0)
    def _():
        previous[...] = jnp.zeros((R * W, C), jnp.bfloat16)

    order = list(reversed(range(F)))
    loads[0].wait()
    loads[1].wait()
    for n, a in enumerate(order):
        values = lbuf[a].reshape(R * W, C).astype(jnp.float32)
        x1[2 + a, 1 : R + 1] = normed_silu(values, g1buf[...]).reshape(R, W, C)
        if n == 0:
            targets = sum(inside(*way).astype(jnp.int32) for way in WAYS)
            pl.semaphore_wait(barrier, targets)
        send(0, x1, a)

    for dt in (2, 1, 0):
        w_loads[1][dt].start()
    loads[3].start()

    loaded = set()

    def conv(k, x, wbuf, a):
        totals = [None] * 3
        for dt in (2, 1, 0):
            if (k, dt) not in loaded:
                loaded.add((k, dt))
                w_loads[k][dt].wait()
            receive(k, x, a + dt)
            cells = jnp.concatenate(
                [x[a + dt, di : di + R].reshape(R * W, C) for di in range(3)], axis=1
            )
            for dj in range(3):
                taps = jnp.concatenate([wbuf[dt, di, dj] for di in range(3)], axis=0)
                part = jnp.dot(cells, taps, preferred_element_type=jnp.float32)
                totals[dj] = part if totals[dj] is None else totals[dj] + part
        return shifted(totals[0], 1, R, W) + totals[1] + shifted(totals[2], -1, R, W)

    for n, a in enumerate(order):
        hidden = conv(0, x1, w1buf, a).astype(jnp.bfloat16).astype(jnp.float32)
        if n == 0:
            loads[2].wait()
        x2[2 + a, 1 : R + 1] = normed_silu(hidden, g2buf[...]).reshape(R, W, C)
        send(1, x2, a)

    last = pltpu.make_async_remote_copy(
        src_ref=blocks.at[F - 1], dst_ref=previous,
        send_sem=last_sem.at[0], recv_sem=last_sem.at[1],
        device_id=there(1, 0), device_id_type=MESH,
    )
    for n, a in enumerate(order):
        total = conv(1, x2, w2buf, a) + lbuf[a].reshape(R * W, C).astype(jnp.float32)
        blocks[a] = total.astype(jnp.bfloat16)
        if n == 0:
            @pl.when(inside(1, 0))
            def _():
                last.start()

    loads[3].wait()

    def put(j, value):
        out[0, j] = value.astype(jnp.bfloat16).reshape(R, W, C)

    def product(rows, m):
        return jnp.dot(rows, ubuf[m], preferred_element_type=jnp.float32)

    for a in order:
        put(2 * a + 1, product(blocks[a], 2))
        if a:
            put(2 * a, product(blocks[a], 0) + product(blocks[a - 1], 1))
    first = product(blocks[0], 0)

    @pl.when(inside(-1, 0))
    def _():
        last.wait_recv()

    put(0, first + product(previous[...], 1))

    for k, x in enumerate((x1, x2)):
        for a in order:
            sent(k, x, a)

    @pl.when(inside(1, 0))
    def _():
        last.wait_send()


def local(tiles, latents, gain_one, conv_one, gain_two, conv_two, upsample):
    videos, F, R, W, C = latents.shape
    assert videos == 1 and F >= 2
    in_hbm = pl.BlockSpec(memory_space=pltpu.HBM)
    bf16, f32 = jnp.bfloat16, jnp.float32
    return pl.pallas_call(
        functools.partial(kernel, tiles),
        out_shape=pltpu.VMEM((1, 2 * F, R, W, C), bf16),
        in_specs=[in_hbm] * 6,
        out_specs=pl.BlockSpec(memory_space=pltpu.VMEM),
        scratch_shapes=[
            pltpu.VMEM((F, R, W, C), bf16),
            pltpu.VMEM((1, C), f32),
            pltpu.VMEM((1, C), f32),
            pltpu.VMEM(conv_one.shape, bf16),
            pltpu.VMEM(conv_two.shape, bf16),
            pltpu.VMEM(upsample.shape, bf16),
            pltpu.VMEM((F + 2, R + 2, W, C), bf16),
            pltpu.VMEM((F + 2, R + 2, W, C), bf16),
            pltpu.VMEM((F, R * W, C), bf16),
            pltpu.VMEM((R * W, C), bf16),
            pltpu.SemaphoreType.DMA((4,)),
            pltpu.SemaphoreType.DMA((3,)),
            pltpu.SemaphoreType.DMA((3,)),
            pltpu.SemaphoreType.DMA((2, F, len(WAYS))),
            pltpu.SemaphoreType.DMA((2, F, len(WAYS))),
            pltpu.SemaphoreType.DMA((2,)),
        ],
        compiler_params=pltpu.CompilerParams(
            collective_id=0, has_side_effects=True, vmem_limit_bytes=56 * 2**20
        ),
        cost_estimate=pl.CostEstimate(
            flops=2 * F * R * W * C * C * 57, bytes_accessed=8 * 2**20, transcendentals=4 * F * R * W * C
        ),
    )(latents, gain_one.reshape(1, C), conv_one, gain_two.reshape(1, C), conv_two, upsample)


def solution(mesh):
    tiles = (mesh.shape["tm"], mesh.shape["space"])
    return jax.shard_map(
        functools.partial(local, tiles),
        mesh=mesh,
        in_specs=(P(None, "tm", "space", None, None), P(), P(), P(), P(), P()),
        out_specs=P(None, "tm", "space", None, None),
        check_vma=False,
    )
```

```python
import functools

import jax
import jax.numpy as jnp
from jax import lax
from jax.experimental import pallas as pl
from jax.experimental.pallas import tpu as pltpu
from jax.sharding import PartitionSpec as P

MESH = pl.DeviceIdType.MESH
WAYS = ((0, 1), (0, -1), (1, 0), (1, 1), (1, -1))


def normed_silu(values, gain):
    mean_square = jnp.mean(values * values, axis=-1, keepdims=True)
    scaled = values * lax.rsqrt(mean_square + 1e-06) * gain
    return (scaled * jax.nn.sigmoid(scaled)).astype(jnp.bfloat16)


def shifted(total, by, rows, width):
    cells, channels = total.shape
    column = lax.broadcasted_iota(jnp.int32, total.shape, 0) % width
    if by > 0:
        return jnp.where(column == 0, 0.0, pltpu.roll(total, 1, 0))
    return jnp.where(column == width - 1, 0.0, pltpu.roll(total, cells - 1, 0))


def kernel(
    tiles, lat, g1, w1, g2, w2, up, out,
    lbuf, g1buf, g2buf, w1buf, w2buf, ubuf, x1, x2, blocks, previous,
    load_sem, w1_sem, w2_sem, send_sem, recv_sem, last_sem,
):
    T, S = tiles
    _, F, R, W, C = lat.shape
    t, s = lax.axis_index("tm"), lax.axis_index("space")

    loads = [
        pltpu.make_async_copy(lat.at[0], lbuf, load_sem.at[0]),
        pltpu.make_async_copy(g1, g1buf, load_sem.at[1]),
        pltpu.make_async_copy(g2, g2buf, load_sem.at[2]),
        pltpu.make_async_copy(up, ubuf, load_sem.at[3]),
    ]
    w_loads = [
        {dt: pltpu.make_async_copy(w.at[dt], buf.at[dt], sem.at[dt]) for dt in (2, 1, 0)}
        for w, buf, sem in ((w1, w1buf, w1_sem), (w2, w2buf, w2_sem))
    ]
    loads[0].start()
    loads[1].start()
    for dt in (2, 1, 0):
        w_loads[0][dt].start()
    loads[2].start()
    for dt in (2, 1, 0):
        w_loads[1][dt].start()
    loads[3].start()

    def inside(dt, ds):
        checks = []
        if dt > 0:
            checks.append(t < T - 1)
        if dt < 0:
            checks.append(t > 0)
        if ds > 0:
            checks.append(s < S - 1)
        if ds < 0:
            checks.append(s > 0)
        return functools.reduce(jnp.logical_and, checks)

    def there(dt, ds):
        return (t + dt, s + ds)

    barrier = pltpu.get_barrier_semaphore()
    for dt, ds in WAYS:
        @pl.when(inside(-dt, -ds))
        def _():
            pl.semaphore_signal(barrier, inc=1, device_id=there(-dt, -ds), device_id_type=MESH)

    def message(k, x, a, way):
        dt, ds = WAYS[way]
        src_rows = {0: pl.ds(1, R), 1: pl.ds(R, 1), -1: pl.ds(1, 1)}[ds]
        dst_rows = {0: pl.ds(1, R), 1: pl.ds(0, 1), -1: pl.ds(R + 1, 1)}[ds]
        dst_frame = a - (F - 2) if dt else 2 + a
        return pltpu.make_async_remote_copy(
            src_ref=x.at[2 + a, src_rows],
            dst_ref=x.at[dst_frame, dst_rows],
            send_sem=send_sem.at[k, a, way],
            recv_sem=recv_sem.at[k, a, way],
            device_id=there(dt, ds),
            device_id_type=MESH,
        )

    def ways_of(a):
        return [way for way, (dt, _) in enumerate(WAYS) if dt == 0 or a >= F - 2]

    def send(k, x, a):
        for way in ways_of(a):
            @pl.when(inside(*WAYS[way]))
            def _():
                message(k, x, a, way).start()

    def sent(k, x, a):
        for way in ways_of(a):
            @pl.when(inside(*WAYS[way]))
            def _():
                message(k, x, a, way).wait_send()

    arrived = set()

    def receive(k, x, frame):
        if (k, frame) in arrived:
            return
        arrived.add((k, frame))
        early = frame < 2
        a = frame + F - 2 if early else frame - 2
        for way in ways_of(a):
            dt, ds = WAYS[way]
            if (dt > 0) == early:
                @pl.when(inside(-dt, -ds))
                def _():
                    message(k, x, a, way).wait_recv()

    zero_row = jnp.zeros((F + 2, 1, W, C), jnp.bfloat16)
    for x in (x1, x2):
        @pl.when(t == 0)
        def _():
            x[0:2] = jnp.zeros((2, R + 2, W, C), jnp.bfloat16)

        @pl.when(s == 0)
        def _():
            x[:, 0:1] = zero_row

        @pl.when(s == S - 1)
        def _():
            x[:, R + 1 : R + 2] = zero_row

    @pl.when(t == 0)
    def _():
        previous[...] = jnp.zeros((R * W, C), jnp.bfloat16)

    order = list(reversed(range(F)))
    loads[0].wait()
    loads[1].wait()
    for n, a in enumerate(order):
        values = lbuf[a].reshape(R * W, C).astype(jnp.float32)
        x1[2 + a, 1 : R + 1] = normed_silu(values, g1buf[...]).reshape(R, W, C)
        if n == 0:
            targets = sum(inside(*way).astype(jnp.int32) for way in WAYS)
            pl.semaphore_wait(barrier, targets)
        send(0, x1, a)

    loaded = set()

    def conv(k, x, wbuf, a):
        totals = [None] * 3
        for dt in (2, 1, 0):
            if (k, dt) not in loaded:
                loaded.add((k, dt))
                w_loads[k][dt].wait()
            receive(k, x, a + dt)
            cells = jnp.concatenate(
                [x[a + dt, di : di + R].reshape(R * W, C) for di in range(3)], axis=1
            )
            for dj in range(3):
                taps = jnp.concatenate([wbuf[dt, di, dj] for di in range(3)], axis=0)
                part = jnp.dot(cells, taps, preferred_element_type=jnp.float32)
                totals[dj] = part if totals[dj] is None else totals[dj] + part
        return shifted(totals[0], 1, R, W) + totals[1] + shifted(totals[2], -1, R, W)

    for n, a in enumerate(order):
        hidden = conv(0, x1, w1buf, a).astype(jnp.bfloat16).astype(jnp.float32)
        if n == 0:
            loads[2].wait()
        x2[2 + a, 1 : R + 1] = normed_silu(hidden, g2buf[...]).reshape(R, W, C)
        send(1, x2, a)

    last = pltpu.make_async_remote_copy(
        src_ref=blocks.at[F - 1], dst_ref=previous,
        send_sem=last_sem.at[0], recv_sem=last_sem.at[1],
        device_id=there(1, 0), device_id_type=MESH,
    )
    for n, a in enumerate(order):
        total = conv(1, x2, w2buf, a) + lbuf[a].reshape(R * W, C).astype(jnp.float32)
        blocks[a] = total.astype(jnp.bfloat16)
        if n == 0:
            @pl.when(inside(1, 0))
            def _():
                last.start()

    loads[3].wait()

    def put(j, value):
        out[0, j] = value.astype(jnp.bfloat16).reshape(R, W, C)

    def product(rows, m):
        return jnp.dot(rows, ubuf[m], preferred_element_type=jnp.float32)

    for a in order:
        put(2 * a + 1, product(blocks[a], 2))
        if a:
            put(2 * a, product(blocks[a], 0) + product(blocks[a - 1], 1))
    first = product(blocks[0], 0)

    @pl.when(inside(-1, 0))
    def _():
        last.wait_recv()

    put(0, first + product(previous[...], 1))

    for k, x in enumerate((x1, x2)):
        for a in order:
            sent(k, x, a)

    @pl.when(inside(1, 0))
    def _():
        last.wait_send()


def local(tiles, latents, gain_one, conv_one, gain_two, conv_two, upsample):
    videos, F, R, W, C = latents.shape
    assert videos == 1 and F >= 2
    in_hbm = pl.BlockSpec(memory_space=pltpu.HBM)
    bf16, f32 = jnp.bfloat16, jnp.float32
    return pl.pallas_call(
        functools.partial(kernel, tiles),
        out_shape=pltpu.VMEM((1, 2 * F, R, W, C), bf16),
        in_specs=[in_hbm] * 6,
        out_specs=pl.BlockSpec(memory_space=pltpu.VMEM),
        scratch_shapes=[
            pltpu.VMEM((F, R, W, C), bf16),
            pltpu.VMEM((1, C), f32),
            pltpu.VMEM((1, C), f32),
            pltpu.VMEM(conv_one.shape, bf16),
            pltpu.VMEM(conv_two.shape, bf16),
            pltpu.VMEM(upsample.shape, bf16),
            pltpu.VMEM((F + 2, R + 2, W, C), bf16),
            pltpu.VMEM((F + 2, R + 2, W, C), bf16),
            pltpu.VMEM((F, R * W, C), bf16),
            pltpu.VMEM((R * W, C), bf16),
            pltpu.SemaphoreType.DMA((4,)),
            pltpu.SemaphoreType.DMA((3,)),
            pltpu.SemaphoreType.DMA((3,)),
            pltpu.SemaphoreType.DMA((2, F, len(WAYS))),
            pltpu.SemaphoreType.DMA((2, F, len(WAYS))),
            pltpu.SemaphoreType.DMA((2,)),
        ],
        compiler_params=pltpu.CompilerParams(
            collective_id=0, has_side_effects=True, vmem_limit_bytes=56 * 2**20
        ),
        cost_estimate=pl.CostEstimate(
            flops=2 * F * R * W * C * C * 57, bytes_accessed=8 * 2**20, transcendentals=4 * F * R * W * C
        ),
    )(latents, gain_one.reshape(1, C), conv_one, gain_two.reshape(1, C), conv_two, upsample)


def solution(mesh):
    tiles = (mesh.shape["tm"], mesh.shape["space"])
    return jax.shard_map(
        functools.partial(local, tiles),
        mesh=mesh,
        in_specs=(P(None, "tm", "space", None, None), P(), P(), P(), P(), P()),
        out_specs=P(None, "tm", "space", None, None),
        check_vma=False,
    )
```

```python
import functools

import jax
import jax.numpy as jnp
from jax import lax
from jax.experimental import pallas as pl
from jax.experimental.pallas import tpu as pltpu
from jax.sharding import PartitionSpec as P

MESH = pl.DeviceIdType.MESH
WAYS = ((1, 0), (1, 1), (1, -1), (0, 1), (0, -1))


def normed_silu(values, gain):
    mean_square = jnp.mean(values * values, axis=-1, keepdims=True)
    scaled = values * lax.rsqrt(mean_square + 1e-06) * gain
    return (scaled * jax.nn.sigmoid(scaled)).astype(jnp.bfloat16)


def shifted(total, by, rows, width):
    cells, channels = total.shape
    column = lax.broadcasted_iota(jnp.int32, total.shape, 0) % width
    if by > 0:
        return jnp.where(column == 0, 0.0, pltpu.roll(total, 1, 0))
    return jnp.where(column == width - 1, 0.0, pltpu.roll(total, cells - 1, 0))


def kernel(
    tiles, lat, g1, w1, g2, w2, up, out,
    lbuf, g1buf, g2buf, w1buf, w2buf, ubuf, x1, x2, blocks, previous,
    load_sem, w1_sem, w2_sem, send_sem, recv_sem, last_sem,
):
    T, S = tiles
    _, F, R, W, C = lat.shape
    t, s = lax.axis_index("tm"), lax.axis_index("space")

    loads = [
        pltpu.make_async_copy(lat.at[0], lbuf, load_sem.at[0]),
        pltpu.make_async_copy(g1, g1buf, load_sem.at[1]),
        pltpu.make_async_copy(g2, g2buf, load_sem.at[2]),
        pltpu.make_async_copy(up, ubuf, load_sem.at[3]),
    ]
    w_loads = [
        {
            dt: [
                pltpu.make_async_copy(w.at[dt, :, dj], buf.at[dt, dj], sem.at[dt, dj])
                for dj in range(3)
            ]
            for dt in (2, 1, 0)
        }
        for w, buf, sem in ((w1, w1buf, w1_sem), (w2, w2buf, w2_sem))
    ]
    loads[0].start()
    loads[1].start()
    for dt in (2, 1, 0):
        for load in w_loads[0][dt]:
            load.start()
    loads[2].start()
    for dt in (2, 1, 0):
        for load in w_loads[1][dt]:
            load.start()
    loads[3].start()

    def inside(dt, ds):
        checks = []
        if dt > 0:
            checks.append(t < T - 1)
        if dt < 0:
            checks.append(t > 0)
        if ds > 0:
            checks.append(s < S - 1)
        if ds < 0:
            checks.append(s > 0)
        return functools.reduce(jnp.logical_and, checks)

    def there(dt, ds):
        return (t + dt, s + ds)

    barrier = pltpu.get_barrier_semaphore()
    for dt, ds in WAYS:
        @pl.when(inside(-dt, -ds))
        def _():
            pl.semaphore_signal(barrier, inc=1, device_id=there(-dt, -ds), device_id_type=MESH)

    def message(k, x, a, way):
        dt, ds = WAYS[way]
        src_rows = {0: pl.ds(1, R), 1: pl.ds(R, 1), -1: pl.ds(1, 1)}[ds]
        dst_rows = {0: pl.ds(1, R), 1: pl.ds(0, 1), -1: pl.ds(R + 1, 1)}[ds]
        dst_frame = a - (F - 2) if dt else 2 + a
        return pltpu.make_async_remote_copy(
            src_ref=x.at[2 + a, src_rows],
            dst_ref=x.at[dst_frame, dst_rows],
            send_sem=send_sem.at[k, a, way],
            recv_sem=recv_sem.at[k, a, way],
            device_id=there(dt, ds),
            device_id_type=MESH,
        )

    def ways_of(a):
        return [way for way, (dt, _) in enumerate(WAYS) if dt == 0 or a >= F - 2]

    def send(k, x, a):
        for way in ways_of(a):
            @pl.when(inside(*WAYS[way]))
            def _():
                message(k, x, a, way).start()

    def sent(k, x, a):
        for way in ways_of(a):
            @pl.when(inside(*WAYS[way]))
            def _():
                message(k, x, a, way).wait_send()

    arrived = set()

    def receive(k, x, frame):
        if (k, frame) in arrived:
            return
        arrived.add((k, frame))
        early = frame < 2
        a = frame + F - 2 if early else frame - 2
        for way in ways_of(a):
            dt, ds = WAYS[way]
            if (dt > 0) == early:
                @pl.when(inside(-dt, -ds))
                def _():
                    message(k, x, a, way).wait_recv()

    zero_row = jnp.zeros((F + 2, 1, W, C), jnp.bfloat16)
    for x in (x1, x2):
        @pl.when(t == 0)
        def _():
            x[0:2] = jnp.zeros((2, R + 2, W, C), jnp.bfloat16)

        @pl.when(s == 0)
        def _():
            x[:, 0:1] = zero_row

        @pl.when(s == S - 1)
        def _():
            x[:, R + 1 : R + 2] = zero_row

    @pl.when(t == 0)
    def _():
        previous[...] = jnp.zeros((R * W, C), jnp.bfloat16)

    order = list(reversed(range(F)))
    loads[0].wait()
    loads[1].wait()
    for n, a in enumerate(order):
        values = lbuf[a].reshape(R * W, C).astype(jnp.float32)
        x1[2 + a, 1 : R + 1] = normed_silu(values, g1buf[...]).reshape(R, W, C)
        if n == 0:
            targets = sum(inside(*way).astype(jnp.int32) for way in WAYS)
            pl.semaphore_wait(barrier, targets)
        send(0, x1, a)

    loaded = set()

    def conv(k, x, wbuf, a):
        totals = [None] * 3
        for dt in (2, 1, 0):
            if (k, dt) not in loaded:
                loaded.add((k, dt))
                for load in w_loads[k][dt]:
                    load.wait()
            receive(k, x, a + dt)
            cells = jnp.concatenate(
                [x[a + dt, di : di + R].reshape(R * W, C) for di in range(3)], axis=1
            )
            for dj in range(3):
                taps = wbuf[dt, dj].reshape(3 * C, C)
                part = jnp.dot(cells, taps, preferred_element_type=jnp.float32)
                totals[dj] = part if totals[dj] is None else totals[dj] + part
        return shifted(totals[0], 1, R, W) + totals[1] + shifted(totals[2], -1, R, W)

    for n, a in enumerate(order):
        hidden = conv(0, x1, w1buf, a).astype(jnp.bfloat16).astype(jnp.float32)
        if n == 0:
            loads[2].wait()
        x2[2 + a, 1 : R + 1] = normed_silu(hidden, g2buf[...]).reshape(R, W, C)
        send(1, x2, a)

    last = pltpu.make_async_remote_copy(
        src_ref=blocks.at[F - 1], dst_ref=previous,
        send_sem=last_sem.at[0], recv_sem=last_sem.at[1],
        device_id=there(1, 0), device_id_type=MESH,
    )
    for n, a in enumerate(order):
        total = conv(1, x2, w2buf, a) + lbuf[a].reshape(R * W, C).astype(jnp.float32)
        blocks[a] = total.astype(jnp.bfloat16)
        if n == 0:
            @pl.when(inside(1, 0))
            def _():
                last.start()

    loads[3].wait()

    def put(j, value):
        out[0, j] = value.astype(jnp.bfloat16).reshape(R, W, C)

    def product(rows, m):
        return jnp.dot(rows, ubuf[m], preferred_element_type=jnp.float32)

    for a in order:
        put(2 * a + 1, product(blocks[a], 2))
        if a:
            put(2 * a, product(blocks[a], 0) + product(blocks[a - 1], 1))
    first = product(blocks[0], 0)

    @pl.when(inside(-1, 0))
    def _():
        last.wait_recv()

    put(0, first + product(previous[...], 1))

    for k, x in enumerate((x1, x2)):
        for a in order:
            sent(k, x, a)

    @pl.when(inside(1, 0))
    def _():
        last.wait_send()


def local(tiles, latents, gain_one, conv_one, gain_two, conv_two, upsample):
    videos, F, R, W, C = latents.shape
    assert videos == 1 and F >= 2
    in_hbm = pl.BlockSpec(memory_space=pltpu.HBM)
    bf16, f32 = jnp.bfloat16, jnp.float32
    return pl.pallas_call(
        functools.partial(kernel, tiles),
        out_shape=pltpu.VMEM((1, 2 * F, R, W, C), bf16),
        in_specs=[in_hbm] * 6,
        out_specs=pl.BlockSpec(memory_space=pltpu.VMEM),
        scratch_shapes=[
            pltpu.VMEM((F, R, W, C), bf16),
            pltpu.VMEM((1, C), f32),
            pltpu.VMEM((1, C), f32),
            pltpu.VMEM(conv_one.shape, bf16),
            pltpu.VMEM(conv_two.shape, bf16),
            pltpu.VMEM(upsample.shape, bf16),
            pltpu.VMEM((F + 2, R + 2, W, C), bf16),
            pltpu.VMEM((F + 2, R + 2, W, C), bf16),
            pltpu.VMEM((F, R * W, C), bf16),
            pltpu.VMEM((R * W, C), bf16),
            pltpu.SemaphoreType.DMA((4,)),
            pltpu.SemaphoreType.DMA((3, 3)),
            pltpu.SemaphoreType.DMA((3, 3)),
            pltpu.SemaphoreType.DMA((2, F, len(WAYS))),
            pltpu.SemaphoreType.DMA((2, F, len(WAYS))),
            pltpu.SemaphoreType.DMA((2,)),
        ],
        compiler_params=pltpu.CompilerParams(
            collective_id=0, has_side_effects=True, vmem_limit_bytes=56 * 2**20
        ),
        cost_estimate=pl.CostEstimate(
            flops=2 * F * R * W * C * C * 57, bytes_accessed=8 * 2**20, transcendentals=4 * F * R * W * C
        ),
    )(latents, gain_one.reshape(1, C), conv_one, gain_two.reshape(1, C), conv_two, upsample)


def solution(mesh):
    tiles = (mesh.shape["tm"], mesh.shape["space"])
    return jax.shard_map(
        functools.partial(local, tiles),
        mesh=mesh,
        in_specs=(P(None, "tm", "space", None, None), P(), P(), P(), P(), P()),
        out_specs=P(None, "tm", "space", None, None),
        check_vma=False,
    )
```
